768 devices in a mesh: space: 64 (over x, y, core), mp: 12 (over z).
Axes of the slice: x: 4, y: 8, z: 12, core: 2. Of those that a mesh axis runs over, the one named last changes fastest.
Arguments:
- tokens: bfloat16 [98304, 1024], P('space')
- norm_gain: float32 [1024], replicated, may hold values from 0.5 to 1.5
- w_qkv: bfloat16 [1024, 12, 192], P(None, 'mp')
- w_out: bfloat16 [768, 1024], replicated, may hold values from -0.75 to 0.75
- head_scale: float32 [12], P('mp'), may hold values from 8 to 400
- cycle_to_nested: int32 [98304], P('space'), may hold values from 0 to 98303, as said below
- neighbours: int32 [768, 9], P('space'), may hold values from -1 to 767, as said below
Outputs:
- mixed: bfloat16 [98304, 1024], P(('space', 'mp'))
The draws below stay inside these ranges and needn't reach their ends.
Inputs may be any that keep to these rules, and one draw needn't show every extreme that they name: `cycle_to_nested`: A permutation of the tokens; the cycle rows of each index of space hold exactly 24 of the nested places of each index of space, the block of 1536 places of that index. `neighbours`: slot 0 names the block itself; the other slots name distinct other blocks at most 6 places away in block order, counted around the end of the order; only slots 7 and 8 may be -1.
All inputs are finite; a program needn't handle non-finite values.
Results may differ from the reference program's by a relative error of at most 0.012.
The reference program's roundings to bfloat16 on the way count: a program that leaves them out, or rounds other values in their place, can miss the bound.
Values may be sent and summed in bfloat16 or wider, within the bound.
A program may use at most 32 MiB of HBM per device.

```python
import math
import jax
import jax.numpy as jnp
from jax import lax

D = 1024
HD = 64
BLOCK = 128
NEIGH = 9
REACH = 6
HEADS = 12
TOK_DEV = 1536
TOKENS = 98304
NBLK = 768


def draw_tokens(key, part):
    gathered_key_rows = jax.random.split(jax.random.fold_in(key, 1), 2)
    base = jax.random.normal(gathered_key_rows[0], (TOKENS, D), jnp.float32)
    row_scale = jnp.exp(jax.random.uniform(gathered_key_rows[1], (TOKENS, 1), jnp.float32, 0.0, math.log(10.0)))
    values = base * row_scale
    return values.astype(jnp.bfloat16)


def draw_w_qkv(key, part):
    gathered_key_rows = jax.random.split(jax.random.fold_in(key, 2), 3)
    spread = D ** (-0.5)
    w_query = jax.random.normal(gathered_key_rows[0], (D, HEADS, HD), jnp.float32) * spread
    w_value = jax.random.normal(gathered_key_rows[2], (D, HEADS, HD), jnp.float32) * spread
    noise = jax.random.normal(gathered_key_rows[1], (D, HEADS, HD), jnp.float32) * spread
    w_key = noise
    return jnp.concatenate([w_query, w_key, w_value], axis=2).astype(jnp.bfloat16)


def draw_head_scale(key, part):
    sample = jax.random.uniform(jax.random.fold_in(key, 3), (HEADS,), jnp.float32)
    lower, upper = (math.log(8.0), math.log(40.0))
    return jnp.exp(lower + (upper - lower) * sample)


def draw_cycle_to_nested(key, part):
    device_count = TOKENS // TOK_DEV
    group_rows = TOK_DEV // device_count
    gathered_key_rows = jax.random.split(jax.random.fold_in(key, 4), 2)
    first_keys = jax.random.split(gathered_key_rows[0], device_count)
    second_keys = jax.random.split(gathered_key_rows[1], device_count)
    source_perm = jax.vmap(lambda one_key: jax.random.permutation(one_key, TOK_DEV))(first_keys)
    target_perm = jax.vmap(lambda one_key: jax.random.permutation(one_key, TOK_DEV))(second_keys)
    source_ids = jnp.arange(device_count, dtype=jnp.int32)[:, None]
    target_dev = source_perm // group_rows
    within = source_perm % group_rows
    place = target_perm[target_dev, source_ids * group_rows + within]
    return (target_dev * TOK_DEV + place).reshape(-1).astype(jnp.int32)


def draw_neighbours(key, part):
    gathered_key_rows = jax.random.split(jax.random.fold_in(key, 5), 2)
    offsets = jnp.concatenate([jnp.arange(-REACH, 0, dtype=jnp.int32), jnp.arange(1, REACH + 1, dtype=jnp.int32)])
    ranking = jax.random.randint(gathered_key_rows[0], (NBLK, 2 * REACH), 0, 1 << 20) * (2 * REACH) + jnp.arange(2 * REACH, dtype=jnp.int32)[None, :]
    picked = jnp.argsort(ranking, axis=1)[:, :NEIGH - 1]
    chosen = offsets[picked]
    block_ids = jnp.arange(NBLK, dtype=jnp.int32)[:, None]
    others = jnp.mod(block_ids + chosen, NBLK)
    full = jnp.concatenate([block_ids, others], axis=1)
    corner = (jax.random.randint(gathered_key_rows[1], (NBLK,), 0, 16) == 0) | (jnp.arange(NBLK) == 0)
    dropped = corner[:, None] & (jnp.arange(NEIGH)[None, :] >= NEIGH - 2)
    return jnp.where(dropped, -1, full).astype(jnp.int32)


def centred(key, shape, deviation, limit, kind=jnp.bfloat16):
    values = jax.random.normal(key, shape, jnp.float32) * deviation
    return jnp.minimum(jnp.maximum(values, -limit), limit).astype(kind)


def setup_inputs(seed: int = 0) -> dict:
    streams_of = jax.random.split(jax.random.key(seed), 8)
    return {
        "tokens": draw_tokens(jax.random.fold_in(streams_of[7], 71), 0),
        "norm_gain": jnp.clip(1.0 + 0.1 * jax.random.normal(streams_of[1], (D,), jnp.float32), 0.5, 1.5),
        "w_qkv": draw_w_qkv(jax.random.fold_in(streams_of[7], 71), 0),
        "w_out": centred(streams_of[3], (HEADS * HD, D), HD ** -0.5, 0.75),
        "head_scale": draw_head_scale(jax.random.fold_in(streams_of[7], 71), 0),
        "cycle_to_nested": draw_cycle_to_nested(jax.random.fold_in(streams_of[7], 71), 0),
        "neighbours": draw_neighbours(jax.random.fold_in(streams_of[7], 71), 0),
    }


def norm_rows(tokens, norm_gain):
    values = tokens.astype(jnp.float32)
    mean_square = lax.optimization_barrier(jnp.mean(values * values, axis=1, keepdims=True))
    return (values * lax.rsqrt(mean_square + 1e-05) * norm_gain).astype(jnp.bfloat16)

def project_head(normed, weight_head, scale_value, head_dim):
    projected = jnp.dot(normed, weight_head, preferred_element_type=jnp.float32)
    query_rows = projected[:, :head_dim]
    key_raw = projected[:, head_dim:2 * head_dim]
    values = projected[:, 2 * head_dim:]
    query_rows = query_rows * (scale_value * lax.rsqrt(lax.optimization_barrier(jnp.sum(query_rows * query_rows, axis=1, keepdims=True)) + 1e-06))
    key_raw = key_raw * lax.rsqrt(lax.optimization_barrier(jnp.sum(key_raw * key_raw, axis=1, keepdims=True)) + 1e-06)
    return jnp.concatenate([query_rows, key_raw, values], axis=1).astype(jnp.bfloat16)

def attend_blocks(query_rows, kv_blocks, positions, present, head_dim):
    block_rows = query_rows.shape[1]
    gathered = kv_blocks[positions]
    batch_blocks = gathered.shape[0]
    gathered_key_rows = gathered[..., :head_dim].reshape(batch_blocks, -1, head_dim)
    gathered_value_rows = gathered[..., head_dim:].reshape(batch_blocks, -1, head_dim)
    score_matrix = jnp.einsum('ltv,lpv->ltp', query_rows.astype(jnp.float32), gathered_key_rows.astype(jnp.float32))
    key_mask = jnp.repeat(present, block_rows, axis=1)[:, None, :]
    score_matrix = jnp.where(key_mask, score_matrix, -1e+30)
    row_max = lax.optimization_barrier(jnp.max(score_matrix, axis=2, keepdims=True))
    exponent = jnp.exp(score_matrix - row_max)
    row_total = lax.optimization_barrier(jnp.sum(exponent, axis=2, keepdims=True))
    attention_weight = exponent.astype(jnp.bfloat16)
    weighted_sum = jnp.einsum('uct,uth->uch', attention_weight.astype(jnp.float32), gathered_value_rows.astype(jnp.float32))
    return (weighted_sum / row_total).astype(jnp.bfloat16)

def reference(tokens, norm_gain, w_qkv, w_out, head_scale, cycle_to_nested, neighbours):
    normed = norm_rows(tokens, norm_gain)
    present = neighbours >= 0
    positions = jnp.where(present, neighbours, 0).astype(jnp.int32)

    def one_head(head):
        weight_head = lax.dynamic_index_in_dim(w_qkv, head, 1, keepdims=False)
        packed = project_head(normed, weight_head, head_scale[head], HD)
        nested_ordering = jnp.zeros_like(packed).at[cycle_to_nested].set(packed)
        query_rows = nested_ordering[:, :HD].reshape(NBLK, BLOCK, HD)
        kv_blocks = nested_ordering[:, HD:].reshape(NBLK, BLOCK, 2 * HD)

        def one_block(item):
            query_block, block_pos, block_present = item
            return attend_blocks(query_block[None], kv_blocks, block_pos[None], block_present[None], HD)[0]
        outputs = lax.map(one_block, (query_rows, positions, present), batch_size=64)
        return outputs.reshape(TOKENS, HD)
    heads_out = lax.map(one_head, jnp.arange(HEADS, dtype=jnp.int32))
    attn = jnp.transpose(heads_out, (1, 0, 2)).reshape(TOKENS, HEADS * HD)
    return jnp.dot(attn, w_out, preferred_element_type=jnp.float32).astype(jnp.bfloat16)
```

```python
import functools
import jax
import jax.numpy as jnp
from jax import lax
from jax.experimental import pallas as pl
from jax.experimental.pallas import tpu as pltpu
from jax.sharding import PartitionSpec as P

BLOCK = 128
REACH = 6
MASKED = 2
F32 = jnp.float32
BF16 = jnp.bfloat16
MESH = pl.DeviceIdType.MESH
NT = (((1,), (1,)), ((), ()))


def far_first(size, step):
    half = step // 2
    return jnp.where(step % 2 == 1, size // 2 - 1 - half, size // 2 + half) if size > 1 else 0 * step


def split_space(size):
    across = 4 if size == 64 else size // 4
    return across, size // 2 // across


def kernel(
    dims, tok_hbm, gain_ref, w_ref, wout_hbm, scale_ref, cyc_ref, nb_ref, out_ref,
    tok, wout, packed, place, send, recv, acc, query, keyval, attn, heads,
    tok_sem, wout_sem, ssem, rsem, hsem, grem, asem, arem,
):
    space, mp, reach = dims
    nx, ny = split_space(space)
    rows_dev, width = tok_hbm.shape
    hd = w_ref.shape[1] // 3
    group = rows_dev // space
    blocks = rows_dev // BLOCK
    nblk = blocks * space
    neigh = nb_ref.shape[1]
    tile = min(256, rows_dev)
    tiles = rows_dev // tile
    batch = min(16, space)
    batches = space // batch

    me, head = lax.axis_index("space"), lax.axis_index("mp")
    core, my_y, my_x = me % 2, (me // 2) % ny, me // (2 * ny)

    def displaced(j, sign):
        dc = far_first(2, j % 2)
        dx = far_first(nx, (j // 2) % nx)
        dy = far_first(ny, j // (2 * nx))
        x = (my_x + sign * dx + nx) % nx
        y = (my_y + sign * dy + ny) % ny
        return (x * ny + y) * 2 + (core + dc) % 2

    def ring(t):
        return (head + far_first(mp, t)) % mp

    def token_copy(i):
        part = pl.ds(pl.multiple_of(i * tile, tile), tile)
        return pltpu.make_async_copy(tok_hbm.at[part], tok.at[part], tok_sem.at[i])

    def exchange(j):
        return pltpu.make_async_remote_copy(
            src_ref=send.at[j], dst_ref=recv.at[j], send_sem=ssem.at[j], recv_sem=rsem.at[j],
            device_id=(displaced(j, 1), head), device_id_type=MESH,
        )

    def halo(side):
        if side == 0:
            src, dst, to = keyval.at[pl.ds(reach, reach)], keyval.at[pl.ds(reach + blocks, reach)], me + space - 1
        else:
            src, dst, to = keyval.at[pl.ds(blocks, reach)], keyval.at[pl.ds(0, reach)], me + 1
        return pltpu.make_async_remote_copy(
            src_ref=src, dst_ref=dst, send_sem=hsem.at[side], recv_sem=grem.at[side],
            device_id=(to % space, head), device_id_type=MESH,
        )

    def output_copy(t):
        return pltpu.make_async_remote_copy(
            src_ref=attn.at[t], dst_ref=heads.at[head], send_sem=asem.at[t], recv_sem=arem.at[t],
            device_id=(me, ring(t)), device_id_type=MESH,
        )

    def each(start, stop, body):
        lax.fori_loop(start, stop, lambda i, carry: (body(i), carry)[1], 0)

    barrier = pltpu.get_barrier_semaphore()
    each(0, space - 1, lambda j: pl.semaphore_signal(barrier, inc=1, device_id=(displaced(j, 1), head), device_id_type=MESH))
    each(0, mp - 1, lambda t: pl.semaphore_signal(barrier, inc=1, device_id=(me, ring(t)), device_id_type=MESH))

    each(0, tiles, lambda i: token_copy(i).start())
    wout_copy = pltpu.make_async_copy(wout_hbm, wout, wout_sem)
    wout_copy.start()

    step_ids = lax.broadcasted_iota(jnp.int32, (space, tile), 0)
    targets = displaced(step_ids, 1)
    before = jnp.where(
        lax.broadcasted_iota(jnp.int32, (tile, tile), 0) < lax.broadcasted_iota(jnp.int32, (tile, tile), 1), 1.0, 0.0
    ).astype(BF16)
    offset = step_ids.astype(F32) * group
    for i in range(tiles):
        cyc = cyc_ref[:, i * tile : (i + 1) * tile].astype(F32)
        owner = jnp.floor((cyc + 0.5) * (1.0 / rows_dev)).astype(jnp.int32)
        chosen = jnp.where(targets == owner, 1.0, 0.0)
        ahead = jnp.dot(chosen.astype(BF16), before, preferred_element_type=F32) + offset
        place[:, i * tile : (i + 1) * tile] = jnp.sum(chosen * ahead, axis=0, keepdims=True)
        offset = offset + jnp.sum(chosen, axis=1, keepdims=True)

    weight = w_ref[...]
    weight = jnp.concatenate([weight[:, hd:], weight[:, :hd], jnp.zeros((width, 2 * BLOCK - 3 * hd), BF16)], axis=1)
    lane = lax.broadcasted_iota(jnp.int32, (tile, BLOCK), 1)
    gain = gain_ref[...]
    scale = scale_ref[0]

    def project(i):
        token_copy(i).wait()
        part = pl.ds(pl.multiple_of(i * tile, tile), tile)
        values = tok[part].astype(F32)
        mean_square = jnp.mean(values * values, axis=1, keepdims=True)
        normed = (values * lax.rsqrt(mean_square + 1e-05) * gain).astype(BF16)
        projected = jnp.dot(normed, weight, preferred_element_type=F32)
        kv, q = projected[:, :BLOCK], projected[:, BLOCK:]
        key_square = jnp.sum(jnp.where(lane < hd, kv * kv, 0.0), axis=1, keepdims=True)
        kv = kv * jnp.where(lane < hd, lax.rsqrt(key_square + 1e-06), 1.0)
        q = q * (scale * lax.rsqrt(jnp.sum(q * q, axis=1, keepdims=True) + 1e-06))
        cyc = cyc_ref[:, part].astype(F32)
        cyc = jnp.concatenate(
            [jnp.broadcast_to(cyc[:, r : r + BLOCK], (BLOCK, BLOCK)).T for r in range(0, tile, BLOCK)], axis=0
        )
        slot = cyc - rows_dev * jnp.floor((cyc + 0.5) * (1.0 / rows_dev))
        upper = jnp.floor(slot * (1.0 / 64))
        q = jnp.where(lane == hd, upper, jnp.where(lane == hd + 1, slot - 64 * upper, q))
        packed[part] = jnp.concatenate([kv, q], axis=1).astype(BF16)

    each(0, tiles, project)

    def batch_of(g):
        rows = batch * group
        index = (lax.broadcasted_iota(jnp.int32, (rows, rows_dev), 0) + g * rows).astype(F32)
        pick = jnp.where(index == place[...], 1.0, 0.0).astype(BF16)
        ordered = jnp.dot(pick, packed[...], preferred_element_type=F32)
        parts = [ordered[:, :BLOCK].reshape(batch, group, BLOCK), ordered[:, BLOCK:].reshape(batch, group, BLOCK)]
        send[pl.ds(g * batch, batch)] = jnp.concatenate(parts, axis=1).astype(BF16)

    for g in range(batches):
        batch_of(g)
        if g == 0:
            pl.semaphore_wait(barrier, space - 1 + mp - 1)
        each(g * batch, min((g + 1) * batch, space - 1), lambda j: exchange(j).start())
    recv[space - 1] = send[space - 1]

    rows = batch * group
    lane8 = lax.broadcasted_iota(jnp.int32, (8, BLOCK), 1)
    decode = jnp.where(lane8 == hd, 64.0, jnp.where(lane8 == hd + 1, 1.0, 0.0)).astype(BF16)
    per_tile = tile // BLOCK
    for g in range(batches):
        each(g * batch, min((g + 1) * batch, space - 1), lambda j: exchange(j).wait_recv())
        got = recv[pl.ds(g * batch, batch)].astype(F32)
        kv = got[:, :group].reshape(rows, BLOCK)
        q = got[:, group:].reshape(rows, BLOCK)
        slot = lax.dot_general(decode, q.astype(BF16), NT, preferred_element_type=F32)[:1]
        got = jnp.concatenate([kv, q], axis=1).astype(BF16)
        for i in range(tiles):
            part = pl.ds(i * tile, tile)
            index = (lax.broadcasted_iota(jnp.int32, (tile, rows), 0) + i * tile).astype(F32)
            pick = jnp.where(index == slot, 1.0, 0.0).astype(BF16)
            found = jnp.dot(pick, got, preferred_element_type=F32)
            if g > 0:
                found = acc[part] + found
            if g < batches - 1:
                acc[part] = found
            else:
                kv = found[:, :BLOCK].astype(BF16)
                q = jnp.where(lane < hd, found[:, BLOCK:], 0.0).astype(BF16)
                keyval[pl.ds(reach + i * per_tile, per_tile)] = kv.reshape(per_tile, BLOCK, BLOCK)
                query[pl.ds(i * per_tile, per_tile)] = q.reshape(per_tile, BLOCK, BLOCK)
                if (i + 1) * per_tile >= reach > i * per_tile:
                    halo(0).start()
    halo(1).start()
    halo(0).wait_recv()
    halo(1).wait_recv()

    lane_half = lax.broadcasted_iota(jnp.int32, (BLOCK // 2, BLOCK), 1)

    def attend(b):
        kvs, absent = [], []
        for s in range(neigh):
            nb = nb_ref[b, s]
            at = (nb - me * blocks + nblk // 2 + nblk) % nblk - nblk // 2 + reach
            kvs.append(keyval[jnp.clip(jnp.where(nb >= 0, at, 0), 0, blocks + 2 * reach - 1)])
            absent.append(jnp.where(nb >= 0, 0.0, -1e30))
        kvs = jnp.concatenate(kvs, axis=0)
        scores = lax.dot_general(query[b], kvs, NT, preferred_element_type=F32)
        cut = (neigh - MASKED) * BLOCK
        tail = [scores[:, s * BLOCK : (s + 1) * BLOCK] + absent[s] for s in range(neigh - MASKED, neigh)]
        scores = jnp.concatenate([scores[:, :cut], *tail], axis=1)
        weights = jnp.exp(scores - jnp.max(scores, axis=1, keepdims=True))
        total = jnp.sum(weights, axis=1, keepdims=True)
        mixed = jnp.dot(weights.astype(BF16), kvs, preferred_element_type=F32) / total
        half = BLOCK // 2
        return jnp.where(lane_half < hd, pltpu.roll(mixed[:half], hd, 1), mixed[half:]).astype(BF16)

    def attend_send(t):
        attn[t] = attend(ring(t))
        output_copy(t).start()

    each(0, mp - 1, attend_send)
    heads[head] = attend(head)
    wout_copy.wait()
    each(0, mp - 1, lambda t: output_copy(t).wait_recv())

    halves = [], []
    for h in range(0, mp, 2):
        low, high = heads[h].astype(F32), heads[h + 1].astype(F32)
        halves[0].append(jnp.where(lane_half < hd, low, pltpu.roll(high, hd, 1)))
        halves[1].append(jnp.where(lane_half < hd, pltpu.roll(low, hd, 1), high))
    rows_in = jnp.concatenate([jnp.concatenate(part, axis=1) for part in halves], axis=0).astype(BF16)
    out_ref[...] = jnp.dot(rows_in, wout[...], preferred_element_type=F32).astype(BF16)

    each(0, space - 1, lambda j: exchange(j).wait_send())
    halo(0).wait_send()
    halo(1).wait_send()
    each(0, mp - 1, lambda t: output_copy(t).wait_send())


def per_device(reach, tokens, norm_gain, w_qkv, w_out, head_scale, cycle_to_nested, neighbours):
    space, mp = lax.axis_size("space"), lax.axis_size("mp")
    rows, width = tokens.shape
    wide = w_out.shape[1]
    group, blocks = rows // space, rows // BLOCK
    tiles = rows // min(256, rows)
    vmem, smem, anywhere = (pl.BlockSpec(memory_space=m) for m in (pltpu.VMEM, pltpu.SMEM, pl.ANY))
    dma = pltpu.SemaphoreType.DMA
    return pl.pallas_call(
        functools.partial(kernel, (space, mp, reach)),
        out_shape=jax.ShapeDtypeStruct((rows // mp, wide), BF16),
        in_specs=[anywhere, vmem, vmem, anywhere, smem, vmem, smem],
        out_specs=vmem,
        scratch_shapes=[
            pltpu.VMEM(tokens.shape, BF16),
            pltpu.VMEM(w_out.shape, BF16),
            pltpu.VMEM((rows, 2 * BLOCK), BF16),
            pltpu.VMEM((1, rows), F32),
            pltpu.VMEM((space, 2 * group, BLOCK), BF16),
            pltpu.VMEM((space, 2 * group, BLOCK), BF16),
            pltpu.VMEM((rows, 2 * BLOCK), F32),
            pltpu.VMEM((blocks, BLOCK, BLOCK), BF16),
            pltpu.VMEM((blocks + 2 * reach, BLOCK, BLOCK), BF16),
            pltpu.VMEM((mp, BLOCK // 2, BLOCK), BF16),
            pltpu.VMEM((mp, BLOCK // 2, BLOCK), BF16),
            dma((tiles,)), dma, dma((space,)), dma((space,)), dma((2,)), dma((2,)), dma((mp,)), dma((mp,)),
        ],
        compiler_params=pltpu.CompilerParams(collective_id=0, has_side_effects=True, vmem_limit_bytes=56 * 2**20),
    )(
        tokens, norm_gain.reshape(1, width), w_qkv.reshape(width, -1), w_out, head_scale,
        cycle_to_nested.reshape(1, rows), neighbours,
    )


def solution(mesh, reach=REACH):
    placed = (P("space", None), P(), P(None, "mp", None), P(), P("mp"), P("space"), P("space", None))
    return jax.shard_map(
        functools.partial(per_device, reach), mesh=mesh, in_specs=placed, out_specs=P(("space", "mp"), None), check_vma=False
    )
```

```python
import functools
import jax
import jax.numpy as jnp
from jax import lax
from jax.experimental import pallas as pl
from jax.experimental.pallas import tpu as pltpu
from jax.sharding import PartitionSpec as P

BLOCK = 128
REACH = 6
MASKED = 2
F32 = jnp.float32
BF16 = jnp.bfloat16
MESH = pl.DeviceIdType.MESH
NT = (((1,), (1,)), ((), ()))


def far_first(size, step):
    half = step // 2
    if size % 2:
        return (step + 1) % size
    return jnp.where(step % 2 == 1, size // 2 - 1 - half, size // 2 + half) if size > 1 else 0 * step


def split_space(size):
    across = 4 if size == 64 else size // 4
    return across, size // 2 // across


def kernel(
    dims, tok_hbm, gain_ref, w_ref, wout_hbm, scale_ref, cyc_ref, nb_ref, out_ref,
    tok, wout, packed, place, trade, send, recv, acc, query, keyval, attn, heads,
    tok_sem, wout_sem, csem, drem, ssem, rsem, hsem, grem, asem, arem,
):
    space, mp, reach = dims
    nx, ny = split_space(space)
    rows_dev, width = tok_hbm.shape
    hd = w_ref.shape[0] // 3
    group = rows_dev // space
    blocks = rows_dev // BLOCK
    nblk = blocks * space
    neigh = nb_ref.shape[1]
    tile = min(256, rows_dev)
    tiles = rows_dev // tile
    chips = space // 2
    batch = max(1, chips // 4)
    batches = chips // batch
    third = group // 3

    me, head = lax.axis_index("space"), lax.axis_index("mp")
    core, my_y, my_x = me % 2, (me // 2) % ny, me // (2 * ny)

    def displaced(j):
        x = (my_x + far_first(nx, j % nx)) % nx
        y = (my_y + far_first(ny, j // nx)) % ny
        return x * ny + y

    def ring(t):
        return (head + far_first(mp, t)) % mp

    def token_copy(i):
        part = pl.ds(pl.multiple_of(i * tile, tile), tile)
        return pltpu.make_async_copy(tok_hbm.at[part], tok.at[part], tok_sem.at[i])

    def core_trade(g):
        return pltpu.make_async_remote_copy(
            src_ref=trade.at[g], dst_ref=send.at[pl.ds(g * batch, batch), core], send_sem=csem.at[g], recv_sem=drem.at[g],
            device_id=(me + 1 - 2 * core, head), device_id_type=MESH,
        )

    def exchange(j):
        return pltpu.make_async_remote_copy(
            src_ref=send.at[j], dst_ref=recv.at[j], send_sem=ssem.at[j], recv_sem=rsem.at[j],
            device_id=(displaced(j) * 2 + core, head), device_id_type=MESH,
        )

    def halo(side):
        if side == 0:
            src, dst, to = keyval.at[pl.ds(reach, reach)], keyval.at[pl.ds(reach + blocks, reach)], me + space - 1
        else:
            src, dst, to = keyval.at[pl.ds(blocks, reach)], keyval.at[pl.ds(0, reach)], me + 1
        return pltpu.make_async_remote_copy(
            src_ref=src, dst_ref=dst, send_sem=hsem.at[side], recv_sem=grem.at[side],
            device_id=(to % space, head), device_id_type=MESH,
        )

    def output_copy(t):
        return pltpu.make_async_remote_copy(
            src_ref=attn.at[t], dst_ref=heads.at[head], send_sem=asem.at[t], recv_sem=arem.at[t],
            device_id=(me, ring(t)), device_id_type=MESH,
        )

    def each(start, stop, body):
        lax.fori_loop(start, stop, lambda i, carry: (body(i), carry)[1], 0)

    barrier = pltpu.get_barrier_semaphore()
    each(0, chips - 1, lambda j: pl.semaphore_signal(barrier, inc=1, device_id=(displaced(j) * 2 + core, head), device_id_type=MESH))
    pl.semaphore_signal(barrier, inc=1, device_id=((me + 1) % space, head), device_id_type=MESH)
    pl.semaphore_signal(barrier, inc=1, device_id=((me + space - 1) % space, head), device_id_type=MESH)
    each(0, mp - 1, lambda t: pl.semaphore_signal(barrier, inc=1, device_id=(me, ring(t)), device_id_type=MESH))

    each(0, tiles, lambda i: token_copy(i).start())
    wout_copy = pltpu.make_async_copy(wout_hbm, wout, wout_sem)
    wout_copy.start()

    step_ids = lax.broadcasted_iota(jnp.int32, (space, tile), 0)
    targets = displaced(step_ids // (2 * batch) * batch + step_ids % batch) * 2 + (core + 1 - step_ids // batch % 2) % 2
    before = jnp.where(
        lax.broadcasted_iota(jnp.int32, (tile, tile), 0) < lax.broadcasted_iota(jnp.int32, (tile, tile), 1), 1.0, 0.0
    ).astype(BF16)
    offset = step_ids.astype(F32) * group
    for i in range(tiles):
        cyc = cyc_ref[pl.ds(i * tile, tile)].reshape(1, tile).astype(F32)
        owner = jnp.floor((cyc + 0.5) * (1.0 / rows_dev)).astype(jnp.int32)
        chosen = jnp.where(targets == owner, 1.0, 0.0)
        ahead = jnp.dot(chosen.astype(BF16), before, preferred_element_type=F32) + offset
        place[:, i * tile : (i + 1) * tile] = jnp.sum(chosen * ahead, axis=0, keepdims=True)
        offset = offset + jnp.sum(chosen, axis=1, keepdims=True)

    weight = w_ref[...]
    weight = jnp.concatenate([weight[hd:], weight[:hd], jnp.zeros((2 * BLOCK - 3 * hd, width), BF16)], axis=0)
    lane = lax.broadcasted_iota(jnp.int32, (tile, BLOCK), 1)
    gain = gain_ref[...]
    scale = scale_ref[0]

    def project(i):
        token_copy(i).wait()
        part = pl.ds(pl.multiple_of(i * tile, tile), tile)
        values = tok[part].astype(F32)
        mean_square = jnp.mean(values * values, axis=1, keepdims=True)
        normed = (values * lax.rsqrt(mean_square + 1e-05) * gain).astype(BF16)
        projected = lax.dot_general(normed, weight, NT, preferred_element_type=F32)
        kv, q = projected[:, :BLOCK], projected[:, BLOCK:]
        key_square = jnp.sum(jnp.where(lane < hd, kv * kv, 0.0), axis=1, keepdims=True)
        kv = kv * jnp.where(lane < hd, lax.rsqrt(key_square + 1e-06), 1.0)
        q = q * (scale * lax.rsqrt(jnp.sum(q * q, axis=1, keepdims=True) + 1e-06))
        cyc = cyc_ref[part].reshape(1, tile).astype(F32)
        cyc = jnp.concatenate(
            [jnp.broadcast_to(cyc[:, r : r + BLOCK], (BLOCK, BLOCK)).T for r in range(0, tile, BLOCK)], axis=0
        )
        slot = cyc - rows_dev * jnp.floor((cyc + 0.5) * (1.0 / rows_dev))
        upper = jnp.floor(slot * (1.0 / 64))
        q = jnp.where(lane == hd, upper, jnp.where(lane == hd + 1, slot - 64 * upper, q))
        packed[part] = jnp.concatenate([kv, q], axis=1).astype(BF16)

    each(0, tiles, project)

    def spread(values):
        return values.reshape(-1, group, BLOCK)

    def message(kv, q):
        first, second, last = q[:, :third], q[:, third : 2 * third], q[:, 2 * third :]
        lanes = lax.broadcasted_iota(jnp.int32, first.shape, 2)
        pairs = jnp.where(lanes < hd, first, pltpu.roll(second, hd, 2))
        last = jnp.where((lanes == hd + 2) | (lanes == hd + 3), pltpu.roll(first, 2, 2), last)
        last = jnp.where((lanes == hd + 4) | (lanes == hd + 5), pltpu.roll(second, 4, 2), last)
        return jnp.concatenate([kv, pairs, last], axis=1).astype(BF16)

    def from_message(got):
        pairs, last = got[:, group : group + third], got[:, group + third :]
        lanes = lax.broadcasted_iota(jnp.int32, pairs.shape, 2)
        first = jnp.where(lanes < hd, pairs, pltpu.roll(last, BLOCK - 2, 2))
        second = jnp.where(lanes < hd, pltpu.roll(pairs, hd, 2), pltpu.roll(last, BLOCK - 4, 2))
        return got[:, :group], jnp.concatenate([first, second, last], axis=1)

    rows = 2 * batch * group

    def order_rows(g):
        index = (lax.broadcasted_iota(jnp.int32, (rows, rows_dev), 0) + g * rows).astype(F32)
        pick = jnp.where(index == place[...], 1.0, 0.0).astype(BF16)
        ordered = jnp.dot(pick, packed[...], preferred_element_type=F32)
        made = message(spread(ordered[:, :BLOCK]), spread(ordered[:, BLOCK:]))
        trade[g] = made[:batch]
        send[pl.ds(g * batch, batch), core] = made[batch:]

    def send_batch(g):
        core_trade(g).wait_recv()
        each(g * batch, min((g + 1) * batch, chips - 1), lambda j: exchange(j).start())

    for g in range(batches):
        order_rows(g)
        if g == 0:
            pl.semaphore_wait(barrier, chips - 1 + 2 + mp - 1)
        core_trade(g).start()
        if g > 0:
            send_batch(g - 1)
    send_batch(batches - 1)
    recv[chips - 1] = send[chips - 1]

    lane8 = lax.broadcasted_iota(jnp.int32, (8, BLOCK), 1)
    decode = jnp.where(lane8 == hd, 64.0, jnp.where(lane8 == hd + 1, 1.0, 0.0)).astype(BF16)
    per_tile = tile // BLOCK
    for g in range(batches):
        each(g * batch, min((g + 1) * batch, chips - 1), lambda j: exchange(j).wait_recv())
        got = recv[pl.ds(g * batch, batch)].astype(F32)
        kv, q = from_message(got.reshape(2 * batch, group + 2 * third, BLOCK))
        kv, q = kv.reshape(rows, BLOCK), q.reshape(rows, BLOCK)
        slot = lax.dot_general(decode, q.astype(BF16), NT, preferred_element_type=F32)[:1]
        got = jnp.concatenate([kv, q], axis=1).astype(BF16)
        for i in range(tiles):
            part = pl.ds(i * tile, tile)
            index = (lax.broadcasted_iota(jnp.int32, (tile, rows), 0) + i * tile).astype(F32)
            pick = jnp.where(index == slot, 1.0, 0.0).astype(BF16)
            found = jnp.dot(pick, got, preferred_element_type=F32)
            if g > 0:
                found = acc[part] + found
            if g < batches - 1:
                acc[part] = found
            else:
                kv = found[:, :BLOCK].astype(BF16)
                q = jnp.where(lane < hd, found[:, BLOCK:], 0.0).astype(BF16)
                keyval[pl.ds(reach + i * per_tile, per_tile)] = kv.reshape(per_tile, BLOCK, BLOCK)
                query[pl.ds(i * per_tile, per_tile)] = q.reshape(per_tile, BLOCK, BLOCK)
                if (i + 1) * per_tile >= reach > i * per_tile:
                    halo(0).start()
    halo(1).start()
    halo(0).wait_recv()
    halo(1).wait_recv()

    lane_half = lax.broadcasted_iota(jnp.int32, (BLOCK // 2, BLOCK), 1)

    def attend(b):
        kvs, absent = [], []
        for s in range(neigh):
            nb = nb_ref[b, s]
            at = (nb - me * blocks + nblk // 2 + nblk) % nblk - nblk // 2 + reach
            kvs.append(keyval[jnp.clip(jnp.where(nb >= 0, at, 0), 0, blocks + 2 * reach - 1)])
            absent.append(jnp.where(nb >= 0, 0.0, -1e30))
        kvs = jnp.concatenate(kvs, axis=0)
        scores = lax.dot_general(query[b], kvs, NT, preferred_element_type=F32)
        cut = (neigh - MASKED) * BLOCK
        tail = [scores[:, s * BLOCK : (s + 1) * BLOCK] + absent[s] for s in range(neigh - MASKED, neigh)]
        scores = jnp.concatenate([scores[:, :cut], *tail], axis=1)
        weights = jnp.exp(scores - jnp.max(scores, axis=1, keepdims=True))
        total = jnp.sum(weights, axis=1, keepdims=True)
        mixed = jnp.dot(weights.astype(BF16), kvs, preferred_element_type=F32) / total
        half = BLOCK // 2
        return jnp.where(lane_half < hd, pltpu.roll(mixed[:half], hd, 1), mixed[half:]).astype(BF16)

    def attend_send(t):
        attn[t] = attend(ring(t))
        output_copy(t).start()

    each(0, mp - 1, attend_send)
    heads[head] = attend(head)
    wout_copy.wait()
    each(0, mp - 1, lambda t: output_copy(t).wait_recv())

    halves = [], []
    for h in range(0, mp, 2):
        low, high = heads[h].astype(F32), heads[h + 1].astype(F32)
        halves[0].append(jnp.where(lane_half < hd, low, pltpu.roll(high, hd, 1)))
        halves[1].append(jnp.where(lane_half < hd, pltpu.roll(low, hd, 1), high))
    rows_in = jnp.concatenate([jnp.concatenate(part, axis=1) for part in halves], axis=0).astype(BF16)
    out_ref[...] = jnp.dot(rows_in, wout[...], preferred_element_type=F32).astype(BF16)

    each(0, batches, lambda g: core_trade(g).wait_send())
    each(0, chips - 1, lambda j: exchange(j).wait_send())
    halo(0).wait_send()
    halo(1).wait_send()
    each(0, mp - 1, lambda t: output_copy(t).wait_send())


def per_device(reach, tokens, norm_gain, w_qkv, w_out, head_scale, cycle_to_nested, neighbours):
    space, mp = lax.axis_size("space"), lax.axis_size("mp")
    rows, width = tokens.shape
    wide = w_out.shape[1]
    group, blocks = rows // space, rows // BLOCK
    tiles = rows // min(256, rows)
    chips = space // 2
    batch = max(1, chips // 4)
    batches, message = chips // batch, group + 2 * (group // 3)
    vmem, smem, anywhere = (pl.BlockSpec(memory_space=m) for m in (pltpu.VMEM, pltpu.SMEM, pl.ANY))
    dma = pltpu.SemaphoreType.DMA
    return pl.pallas_call(
        functools.partial(kernel, (space, mp, reach)),
        out_shape=jax.ShapeDtypeStruct((rows // mp, wide), BF16),
        in_specs=[anywhere, vmem, vmem, anywhere, smem, vmem, smem],
        out_specs=vmem,
        scratch_shapes=[
            pltpu.VMEM(tokens.shape, BF16),
            pltpu.VMEM(w_out.shape, BF16),
            pltpu.VMEM((rows, 2 * BLOCK), BF16),
            pltpu.VMEM((1, rows), F32),
            pltpu.VMEM((batches, batch, message, BLOCK), BF16),
            pltpu.VMEM((chips, 2, message, BLOCK), BF16),
            pltpu.VMEM((chips, 2, message, BLOCK), BF16),
            pltpu.VMEM((rows, 2 * BLOCK), F32),
            pltpu.VMEM((blocks, BLOCK, BLOCK), BF16),
            pltpu.VMEM((blocks + 2 * reach, BLOCK, BLOCK), BF16),
            pltpu.VMEM((mp, BLOCK // 2, BLOCK), BF16),
            pltpu.VMEM((mp, BLOCK // 2, BLOCK), BF16),
            dma((tiles,)), dma, dma((batches,)), dma((batches,)), dma((chips,)), dma((chips,)), dma((2,)), dma((2,)), dma((mp,)), dma((mp,)),
        ],
        compiler_params=pltpu.CompilerParams(collective_id=0, has_side_effects=True, vmem_limit_bytes=56 * 2**20),
    )(
        tokens, norm_gain.reshape(1, width), w_qkv.transpose(1, 2, 0).reshape(-1, width), w_out, head_scale,
        cycle_to_nested, neighbours,
    )


def solution(mesh, reach=REACH):
    placed = (P("space", None), P(), P(None, "mp", None), P(), P("mp"), P("space"), P("space", None))
    return jax.shard_map(
        functools.partial(per_device, reach), mesh=mesh, in_specs=placed, out_specs=P(("space", "mp"), None), check_vma=False
    )
```

```python
import functools
import jax
import jax.numpy as jnp
from jax import lax
from jax.experimental import pallas as pl
from jax.experimental.pallas import tpu as pltpu
from jax.sharding import PartitionSpec as P

BLOCK = 128
REACH = 6
MASKED = 2
F32 = jnp.float32
BF16 = jnp.bfloat16
MESH = pl.DeviceIdType.MESH
NT = (((1,), (1,)), ((), ()))


def far_static(size, step):
    if size % 2:
        return (step + 1) % size
    return size // 2 - 1 - step // 2 if step % 2 else size // 2 + step // 2


def chip_steps(nx, ny):
    xs = [far_static(nx, i) if nx > 1 else 0 for i in range(nx)]
    steps = [(dx, ny // 2) for dx in xs]
    same = [(dx, 0) for dx in xs if dx]
    for level in range(ny // 2 - 1, 0, -1):
        if level == 1:
            steps += same
        steps += [(dx, dy) for dx in xs for dy in (level, ny - level)]
    return (steps if ny > 2 else steps + same) + [(0, 0)]


def split_space(size):
    across = 4 if size == 64 else size // 4
    return across, size // 2 // across


def kernel(
    dims, tok_hbm, gain_ref, w_ref, wout_hbm, scale_ref, cyc_ref, nb_ref, out_ref,
    tok, wout, packed, place, trade, send, recv, acc, query, keyval, attn, heads, mixed,
    tok_sem, wout_sem, csem, drem, ssem, rsem, hsem, grem, asem, arem,
):
    space, mp, reach = dims
    nx, ny = split_space(space)
    rows_dev, width = tok_hbm.shape
    hd = w_ref.shape[0] // 3
    group = rows_dev // space
    blocks = rows_dev // BLOCK
    nblk = blocks * space
    neigh = nb_ref.shape[1]
    tile = min(256, rows_dev)
    tiles = rows_dev // tile
    chips = space // 2
    batch = max(1, chips // 4)
    batches = chips // batch
    third = group // 3

    me, head = lax.axis_index("space"), lax.axis_index("mp")
    core, my_y, my_x = lax.rem(me, 2), lax.rem(me // 2, ny), me // (2 * ny)
    steps = chip_steps(nx, ny)

    def displaced(j):
        dx, dy = steps[j]
        return lax.rem(my_x + dx, nx) * ny + lax.rem(my_y + dy, ny)

    def ring(t):
        return lax.rem(head + far_static(mp, t), mp)

    def token_copy(i):
        part = pl.ds(pl.multiple_of(i * tile, tile), tile)
        return pltpu.make_async_copy(tok_hbm.at[part], tok.at[part], tok_sem.at[i])

    def core_trade(g):
        return pltpu.make_async_remote_copy(
            src_ref=trade.at[g], dst_ref=send.at[pl.ds(g * batch, batch), core], send_sem=csem.at[g], recv_sem=drem.at[g],
            device_id=(me + 1 - 2 * core, head), device_id_type=MESH,
        )

    def exchange(j):
        return pltpu.make_async_remote_copy(
            src_ref=send.at[j], dst_ref=recv.at[j], send_sem=ssem.at[j], recv_sem=rsem.at[j],
            device_id=(displaced(j) * 2 + core, head), device_id_type=MESH,
        )

    def halo(i):
        per_tile = tile // BLOCK
        low, high = i * per_tile, (i + 1) * per_tile
        pieces = []
        if low < reach:
            pieces.append((low, min(high, reach) - low, low + reach + blocks, me + space - 1))
        if high > blocks - reach:
            first = max(low, blocks - reach)
            pieces.append((first, high - first, first - (blocks - reach), me + 1))
        return [
            pltpu.make_async_remote_copy(
                src_ref=keyval.at[pl.ds(reach + start, count)], dst_ref=keyval.at[pl.ds(to, count)],
                send_sem=hsem.at[i, n], recv_sem=grem.at[i, n], device_id=(who % space, head), device_id_type=MESH,
            )
            for n, (start, count, to, who) in enumerate(pieces)
        ]

    def output_copy(t):
        return pltpu.make_async_remote_copy(
            src_ref=attn.at[t], dst_ref=heads.at[head], send_sem=asem.at[t], recv_sem=arem.at[t],
            device_id=(me, ring(t)), device_id_type=MESH,
        )

    def each(start, stop, body):
        for i in range(start, stop):
            body(i)

    barrier = pltpu.get_barrier_semaphore()
    each(0, chips - 1, lambda j: pl.semaphore_signal(barrier, inc=1, device_id=(displaced(j) * 2 + core, head), device_id_type=MESH))
    pl.semaphore_signal(barrier, inc=1, device_id=((me + 1) % space, head), device_id_type=MESH)
    pl.semaphore_signal(barrier, inc=1, device_id=((me + space - 1) % space, head), device_id_type=MESH)
    each(0, mp - 1, lambda t: pl.semaphore_signal(barrier, inc=1, device_id=(me, ring(t)), device_id_type=MESH))

    each(0, tiles, lambda i: token_copy(i).start())
    wout_copy = pltpu.make_async_copy(wout_hbm, wout, wout_sem)
    wout_copy.start()

    step_ids = lax.broadcasted_iota(jnp.int32, (space, tile), 0)
    targets = jnp.zeros_like(step_ids)
    for j in range(chips):
        start = j // batch * 2 * batch + j % batch
        chip = displaced(j) * 2
        targets = jnp.where(step_ids == start, chip + 1 - core, jnp.where(step_ids == start + batch, chip + core, targets))
    before = jnp.where(
        lax.broadcasted_iota(jnp.int32, (tile, tile), 0) < lax.broadcasted_iota(jnp.int32, (tile, tile), 1), 1.0, 0.0
    ).astype(BF16)
    offset = step_ids.astype(F32) * group
    for i in range(tiles):
        cyc = cyc_ref[pl.ds(i * tile, tile)].reshape(1, tile).astype(F32)
        owner = jnp.floor((cyc + 0.5) * (1.0 / rows_dev)).astype(jnp.int32)
        chosen = jnp.where(targets == owner, 1.0, 0.0)
        ahead = jnp.dot(chosen.astype(BF16), before, preferred_element_type=F32) + offset
        place[:, i * tile : (i + 1) * tile] = jnp.sum(chosen * ahead, axis=0, keepdims=True)
        offset = offset + jnp.sum(chosen, axis=1, keepdims=True)

    weight = w_ref[...]
    weight = jnp.concatenate([weight[hd:], weight[:hd], jnp.zeros((2 * BLOCK - 3 * hd, width), BF16)], axis=0)
    lane = lax.broadcasted_iota(jnp.int32, (tile, BLOCK), 1)
    gain = gain_ref[...]
    scale = scale_ref[0]

    def project(i):
        token_copy(i).wait()
        part = pl.ds(pl.multiple_of(i * tile, tile), tile)
        values = tok[part].astype(F32)
        mean_square = jnp.mean(values * values, axis=1, keepdims=True)
        normed = (values * lax.rsqrt(mean_square + 1e-05) * gain).astype(BF16)
        projected = lax.dot_general(normed, weight, NT, preferred_element_type=F32)
        kv, q = projected[:, :BLOCK], projected[:, BLOCK:]
        key_square = jnp.sum(jnp.where(lane < hd, kv * kv, 0.0), axis=1, keepdims=True)
        kv = kv * jnp.where(lane < hd, lax.rsqrt(key_square + 1e-06), 1.0)
        q = q * (scale * lax.rsqrt(jnp.sum(q * q, axis=1, keepdims=True) + 1e-06))
        cyc = cyc_ref[part].reshape(1, tile).astype(F32)
        cyc = jnp.concatenate(
            [jnp.broadcast_to(cyc[:, r : r + BLOCK], (BLOCK, BLOCK)).T for r in range(0, tile, BLOCK)], axis=0
        )
        slot = cyc - rows_dev * jnp.floor((cyc + 0.5) * (1.0 / rows_dev))
        upper = jnp.floor(slot * (1.0 / 64))
        q = jnp.where(lane == hd, upper, jnp.where(lane == hd + 1, slot - 64 * upper, q))
        packed[part] = jnp.concatenate([kv, q], axis=1).astype(BF16)

    lax.fori_loop(0, tiles, lambda i, carry: (project(i), carry)[1], 0)

    def spread(values):
        return values.reshape(-1, group, BLOCK)

    def message(kv, q):
        first, second, last = q[:, :third], q[:, third : 2 * third], q[:, 2 * third :]
        lanes = lax.broadcasted_iota(jnp.int32, first.shape, 2)
        pairs = jnp.where(lanes < hd, first, pltpu.roll(second, hd, 2))
        last = jnp.where((lanes == hd + 2) | (lanes == hd + 3), pltpu.roll(first, 2, 2), last)
        last = jnp.where((lanes == hd + 4) | (lanes == hd + 5), pltpu.roll(second, 4, 2), last)
        return jnp.concatenate([kv, pairs, last], axis=1).astype(BF16)

    def from_message(got):
        pairs, last = got[:, group : group + third], got[:, group + third :]
        lanes = lax.broadcasted_iota(jnp.int32, pairs.shape, 2)
        first = jnp.where(lanes < hd, pairs, pltpu.roll(last, BLOCK - 2, 2))
        second = jnp.where(lanes < hd, pltpu.roll(pairs, hd, 2), pltpu.roll(last, BLOCK - 4, 2))
        return got[:, :group], jnp.concatenate([first, second, last], axis=1)

    rows = 2 * batch * group

    def order_rows(g):
        index = (lax.broadcasted_iota(jnp.int32, (rows, rows_dev), 0) + g * rows).astype(F32)
        pick = jnp.where(index == place[...], 1.0, 0.0).astype(BF16)
        ordered = jnp.dot(pick, packed[...], preferred_element_type=F32)
        made = message(spread(ordered[:, :BLOCK]), spread(ordered[:, BLOCK:]))
        trade[g] = made[:batch]
        send[pl.ds(g * batch, batch), core] = made[batch:]

    def send_batch(g):
        core_trade(g).wait_recv()
        each(g * batch, min((g + 1) * batch, chips - 1), lambda j: exchange(j).start())

    for g in range(batches):
        order_rows(g)
        if g == 0:
            pl.semaphore_wait(barrier, chips - 1 + 2 + mp - 1)
        core_trade(g).start()
        if g > 0:
            send_batch(g - 1)
    send_batch(batches - 1)
    recv[chips - 1] = send[chips - 1]

    lane8 = lax.broadcasted_iota(jnp.int32, (8, BLOCK), 1)
    decode = jnp.where(lane8 == hd, 64.0, jnp.where(lane8 == hd + 1, 1.0, 0.0)).astype(BF16)
    per_tile = tile // BLOCK
    edges = [g * batch for g in range(batches)] + [chips - batch // 2] * (batch > 1) + [chips]
    centre = [i for n in range((tiles + 1) // 2) for i in dict.fromkeys((n, tiles - 1 - n))]
    for g, (start, stop) in enumerate(zip(edges, edges[1:])):
        each(start, min(stop, chips - 1), lambda j: exchange(j).wait_recv())
        rows = 2 * (stop - start) * group
        got = recv[start:stop].astype(F32)
        kv, q = from_message(got.reshape(-1, group + 2 * third, BLOCK))
        kv, q = kv.reshape(rows, BLOCK), q.reshape(rows, BLOCK)
        slot = lax.dot_general(decode, q.astype(BF16), NT, preferred_element_type=F32)[:1]
        got = jnp.concatenate([kv, q], axis=1).astype(BF16)
        for i in centre:
            part = pl.ds(i * tile, tile)
            index = (lax.broadcasted_iota(jnp.int32, (tile, rows), 0) + i * tile).astype(F32)
            pick = jnp.where(index == slot, 1.0, 0.0).astype(BF16)
            found = jnp.dot(pick, got, preferred_element_type=F32)
            if g > 0:
                found = acc[part] + found
            if stop < chips:
                acc[part] = found
            else:
                kv = found[:, :BLOCK].astype(BF16)
                q = jnp.where(lane < hd, found[:, BLOCK:], 0.0).astype(BF16)
                keyval[pl.ds(reach + i * per_tile, per_tile)] = kv.reshape(per_tile, BLOCK, BLOCK)
                query[pl.ds(i * per_tile, per_tile)] = q.reshape(per_tile, BLOCK, BLOCK)
                for copy in halo(i):
                    copy.start()
    for i in range(tiles):
        for copy in halo(i):
            copy.wait_recv()

    lane_half = lax.broadcasted_iota(jnp.int32, (BLOCK // 2, BLOCK), 1)

    def attend(b):
        kvs, absent = [], []
        for s in range(neigh):
            nb = nb_ref[b, s]
            at = nb - me * blocks + reach
            at = jnp.where(at < 0, at + nblk, jnp.where(at >= blocks + 2 * reach, at - nblk, at))
            kvs.append(keyval[jnp.clip(jnp.where(nb >= 0, at, 0), 0, blocks + 2 * reach - 1)])
            absent.append(jnp.where(nb >= 0, 0.0, -1e30))
        kvs = jnp.concatenate(kvs, axis=0)
        scores = lax.dot_general(query[b], kvs, NT, preferred_element_type=F32)
        cut = (neigh - MASKED) * BLOCK
        tail = [scores[:, s * BLOCK : (s + 1) * BLOCK] + absent[s] for s in range(neigh - MASKED, neigh)]
        scores = jnp.concatenate([scores[:, :cut], *tail], axis=1)
        weights = jnp.exp(scores - jnp.max(scores, axis=1, keepdims=True))
        total = jnp.sum(weights, axis=1, keepdims=True)
        values = jnp.dot(weights.astype(BF16), kvs, preferred_element_type=F32) / total
        half = BLOCK // 2
        return jnp.where(lane_half < hd, pltpu.roll(values[:half], hd, 1), values[half:]).astype(BF16)

    for t in range(0, mp, 2):
        blocks_now = [(step, attend(ring(step))) for step in (t, t + 1)]
        for step, rows_now in blocks_now:
            if step < mp - 1:
                attn[step] = rows_now
                output_copy(step).start()
            else:
                heads[head] = rows_now

    wout_copy.wait()
    for t in range(0, mp, 2):
        came = []
        for step in (t, t + 1):
            if step < mp - 1:
                output_copy(step).wait_recv()
            came.append(lax.rem(head + mp - far_static(mp, step), mp))
        low, high = (heads[h].astype(F32) for h in came)
        top = jnp.where(lane_half < hd, low, pltpu.roll(high, hd, 1))
        bottom = jnp.where(lane_half < hd, pltpu.roll(low, hd, 1), high)
        pair = jnp.concatenate([top, bottom], axis=0).astype(BF16)
        weight = jnp.concatenate([wout[pl.ds(pl.multiple_of(h * hd, hd), hd)] for h in came], axis=0)
        term = jnp.dot(pair, weight, preferred_element_type=F32)
        if t > 0:
            term = mixed[...] + term
        if t < mp - 2:
            mixed[...] = term
        else:
            out_ref[...] = term.astype(BF16)

    each(0, batches, lambda g: core_trade(g).wait_send())
    each(0, chips - 1, lambda j: exchange(j).wait_send())
    for i in range(tiles):
        for copy in halo(i):
            copy.wait_send()
    each(0, mp - 1, lambda t: output_copy(t).wait_send())


def hand_over(mixed_ref, out_ref, sem):
    copy = pltpu.make_async_copy(mixed_ref, out_ref, sem)
    copy.start()
    copy.wait()


def per_device(reach, tokens, norm_gain, w_qkv, w_out, head_scale, cycle_to_nested, neighbours):
    space, mp = lax.axis_size("space"), lax.axis_size("mp")
    rows, width = tokens.shape
    group, blocks = rows // space, rows // BLOCK
    tiles = rows // min(256, rows)
    chips = space // 2
    batch = max(1, chips // 4)
    batches, message = chips // batch, group + 2 * (group // 3)
    vmem, smem, anywhere = (pl.BlockSpec(memory_space=m) for m in (pltpu.VMEM, pltpu.SMEM, pl.ANY))
    dma = pltpu.SemaphoreType.DMA
    mixed = pl.pallas_call(
        functools.partial(kernel, (space, mp, reach)),
        out_shape=jax.ShapeDtypeStruct((rows // mp, w_out.shape[1]), BF16),
        in_specs=[anywhere, vmem, vmem, anywhere, smem, vmem, smem],
        out_specs=vmem,
        scratch_shapes=[
            pltpu.VMEM(tokens.shape, BF16),
            pltpu.VMEM(w_out.shape, BF16),
            pltpu.VMEM((rows, 2 * BLOCK), BF16),
            pltpu.VMEM((1, rows), F32),
            pltpu.VMEM((batches, batch, message, BLOCK), BF16),
            pltpu.VMEM((chips, 2, message, BLOCK), BF16),
            pltpu.VMEM((chips, 2, message, BLOCK), BF16),
            pltpu.VMEM((rows, 2 * BLOCK), F32),
            pltpu.VMEM((blocks, BLOCK, BLOCK), BF16),
            pltpu.VMEM((blocks + 2 * reach, BLOCK, BLOCK), BF16),
            pltpu.VMEM((mp, BLOCK // 2, BLOCK), BF16),
            pltpu.VMEM((mp, BLOCK // 2, BLOCK), BF16),
            pltpu.VMEM((rows // mp, w_out.shape[1]), F32),
            dma((tiles,)), dma, dma((batches,)), dma((batches,)), dma((chips,)), dma((chips,)), dma((tiles, 2)), dma((tiles, 2)), dma((mp,)), dma((mp,)),
        ],
        compiler_params=pltpu.CompilerParams(collective_id=0, has_side_effects=True, vmem_limit_bytes=56 * 2**20),
    )(
        tokens, norm_gain.reshape(1, width), w_qkv.transpose(1, 2, 0).reshape(-1, width), w_out, head_scale,
        cycle_to_nested, neighbours,
    )
    return pl.pallas_call(
        hand_over, out_shape=jax.ShapeDtypeStruct(mixed.shape, BF16), in_specs=[anywhere], out_specs=anywhere, scratch_shapes=[dma]
    )(mixed)


def solution(mesh, reach=REACH):
    placed = (P("space", None), P(), P(None, "mp", None), P(), P("mp"), P("space"), P("space", None))
    return jax.shard_map(
        functools.partial(per_device, reach), mesh=mesh, in_specs=placed, out_specs=P(("space", "mp"), None), check_vma=False
    )
```

```python
import functools
import jax
import jax.numpy as jnp
from jax import lax
from jax.experimental import pallas as pl
from jax.experimental.pallas import tpu as pltpu
from jax.sharding import PartitionSpec as P

BLOCK = 128
REACH = 6
MASKED = 2
F32 = jnp.float32
BF16 = jnp.bfloat16
MESH = pl.DeviceIdType.MESH
NT = (((1,), (1,)), ((), ()))


def far_static(size, step):
    if size % 2:
        return (step + 1) % size
    return size // 2 - 1 - step // 2 if step % 2 else size // 2 + step // 2


def chip_steps(nx, ny):
    xs = [far_static(nx, i) if nx > 1 else 0 for i in range(nx)]
    steps = [(dx, ny // 2) for dx in xs]
    same = [(dx, 0) for dx in xs if dx]
    for level in range(ny // 2 - 1, 0, -1):
        if level == 1:
            steps += same
        steps += [(dx, dy) for dx in xs for dy in (level, ny - level)]
    return (steps if ny > 2 else steps + same) + [(0, 0)]


def split_space(size):
    across = 4 if size == 64 else size // 4
    return across, size // 2 // across


def kernel(
    dims, tok_hbm, gain_ref, w_ref, wout_hbm, scale_ref, cyc_ref, nb_ref, out_ref,
    tok, wout, packed, place, trade, send, recv, acc, query, keyval, attn, heads, mixed,
    tok_sem, wout_sem, csem, drem, ssem, rsem, hsem, grem, asem, arem,
):
    space, mp, reach = dims
    nx, ny = split_space(space)
    rows_dev, width = tok_hbm.shape
    hd = w_ref.shape[0] // 3
    group = rows_dev // space
    blocks = rows_dev // BLOCK
    nblk = blocks * space
    neigh = nb_ref.shape[1]
    tile = min(256, rows_dev)
    tiles = rows_dev // tile
    chips = space // 2
    batch = max(1, chips // 4)
    batches = chips // batch
    third = group // 3

    me, head = lax.axis_index("space"), lax.axis_index("mp")
    core, my_y, my_x = lax.rem(me, 2), lax.rem(me // 2, ny), me // (2 * ny)
    steps = chip_steps(nx, ny)

    def displaced(j):
        dx, dy = steps[j]
        return lax.rem(my_x + dx, nx) * ny + lax.rem(my_y + dy, ny)

    def ring(t):
        return lax.rem(head + far_static(mp, t), mp)

    def token_copy(i):
        part = pl.ds(pl.multiple_of(i * tile, tile), tile)
        return pltpu.make_async_copy(tok_hbm.at[part], tok.at[part], tok_sem.at[i])

    def core_trade(g):
        return pltpu.make_async_remote_copy(
            src_ref=trade.at[g], dst_ref=send.at[pl.ds(g * batch, batch), core], send_sem=csem.at[g], recv_sem=drem.at[g],
            device_id=(me + 1 - 2 * core, head), device_id_type=MESH,
        )

    def exchange(j):
        return pltpu.make_async_remote_copy(
            src_ref=send.at[j], dst_ref=recv.at[j], send_sem=ssem.at[j], recv_sem=rsem.at[j],
            device_id=(displaced(j) * 2 + core, head), device_id_type=MESH,
        )

    def halo(i):
        per_tile = tile // BLOCK
        low, high = i * per_tile, (i + 1) * per_tile
        pieces = []
        if low < reach:
            pieces.append((low, min(high, reach) - low, low + reach + blocks, me + space - 1))
        if high > blocks - reach:
            first = max(low, blocks - reach)
            pieces.append((first, high - first, first - (blocks - reach), me + 1))
        return [
            pltpu.make_async_remote_copy(
                src_ref=keyval.at[pl.ds(reach + start, count)], dst_ref=keyval.at[pl.ds(to, count)],
                send_sem=hsem.at[i, n], recv_sem=grem.at[i, n], device_id=(who % space, head), device_id_type=MESH,
            )
            for n, (start, count, to, who) in enumerate(pieces)
        ]

    def output_copy(t):
        return pltpu.make_async_remote_copy(
            src_ref=attn.at[t], dst_ref=heads.at[head], send_sem=asem.at[t], recv_sem=arem.at[t],
            device_id=(me, ring(t)), device_id_type=MESH,
        )

    def each(start, stop, body):
        for i in range(start, stop):
            body(i)

    barrier = pltpu.get_barrier_semaphore()
    each(0, chips - 1, lambda j: pl.semaphore_signal(barrier, inc=1, device_id=(displaced(j) * 2 + core, head), device_id_type=MESH))
    pl.semaphore_signal(barrier, inc=1, device_id=((me + 1) % space, head), device_id_type=MESH)
    pl.semaphore_signal(barrier, inc=1, device_id=((me + space - 1) % space, head), device_id_type=MESH)
    each(0, mp - 1, lambda t: pl.semaphore_signal(barrier, inc=1, device_id=(me, ring(t)), device_id_type=MESH))

    each(0, tiles, lambda i: token_copy(i).start())
    wout_copy = pltpu.make_async_copy(wout_hbm, wout, wout_sem)
    wout_copy.start()

    step_ids = lax.broadcasted_iota(jnp.int32, (space, tile), 0)
    targets = jnp.zeros_like(step_ids)
    for j in range(chips):
        start = j // batch * 2 * batch + j % batch
        chip = displaced(j) * 2
        targets = jnp.where(step_ids == start, chip + 1 - core, jnp.where(step_ids == start + batch, chip + core, targets))
    before = jnp.where(
        lax.broadcasted_iota(jnp.int32, (tile, tile), 0) < lax.broadcasted_iota(jnp.int32, (tile, tile), 1), 1.0, 0.0
    ).astype(BF16)
    offset = step_ids.astype(F32) * group
    for i in range(tiles):
        cyc = cyc_ref[pl.ds(i * tile, tile)].reshape(1, tile).astype(F32)
        owner = jnp.floor((cyc + 0.5) * (1.0 / rows_dev)).astype(jnp.int32)
        chosen = jnp.where(targets == owner, 1.0, 0.0)
        ahead = jnp.dot(chosen.astype(BF16), before, preferred_element_type=F32) + offset
        place[:, i * tile : (i + 1) * tile] = jnp.sum(chosen * ahead, axis=0, keepdims=True)
        offset = offset + jnp.sum(chosen, axis=1, keepdims=True)

    weight = w_ref[...]
    weight = jnp.concatenate([weight[hd:], weight[:hd], jnp.zeros((2 * BLOCK - 3 * hd, width), BF16)], axis=0)
    lane = lax.broadcasted_iota(jnp.int32, (tile, BLOCK), 1)
    gain = gain_ref[...]
    scale = scale_ref[0]

    def project(i):
        token_copy(i).wait()
        part = pl.ds(pl.multiple_of(i * tile, tile), tile)
        values = tok[part].astype(F32)
        mean_square = jnp.mean(values * values, axis=1, keepdims=True)
        normed = (values * lax.rsqrt(mean_square + 1e-05) * gain).astype(BF16)
        projected = lax.dot_general(normed, weight, NT, preferred_element_type=F32)
        kv, q = projected[:, :BLOCK], projected[:, BLOCK:]
        key_square = jnp.sum(jnp.where(lane < hd, kv * kv, 0.0), axis=1, keepdims=True)
        kv = kv * jnp.where(lane < hd, lax.rsqrt(key_square + 1e-06), 1.0)
        q = q * (scale * lax.rsqrt(jnp.sum(q * q, axis=1, keepdims=True) + 1e-06))
        cyc = cyc_ref[part].reshape(1, tile).astype(F32)
        cyc = jnp.concatenate(
            [jnp.broadcast_to(cyc[:, r : r + BLOCK], (BLOCK, BLOCK)).T for r in range(0, tile, BLOCK)], axis=0
        )
        slot = cyc - rows_dev * jnp.floor((cyc + 0.5) * (1.0 / rows_dev))
        upper = jnp.floor(slot * (1.0 / 64))
        q = jnp.where(lane == hd, upper, jnp.where(lane == hd + 1, slot - 64 * upper, q))
        packed[part] = jnp.concatenate([kv, q], axis=1).astype(BF16)

    lax.fori_loop(0, tiles, lambda i, carry: (project(i), carry)[1], 0)

    def spread(values):
        return values.reshape(-1, group, BLOCK)

    def message(kv, q):
        first, second, last = q[:, :third], q[:, third : 2 * third], q[:, 2 * third :]
        lanes = lax.broadcasted_iota(jnp.int32, first.shape, 2)
        pairs = jnp.where(lanes < hd, first, pltpu.roll(second, hd, 2))
        last = jnp.where((lanes == hd + 2) | (lanes == hd + 3), pltpu.roll(first, 2, 2), last)
        last = jnp.where((lanes == hd + 4) | (lanes == hd + 5), pltpu.roll(second, 4, 2), last)
        return jnp.concatenate([kv, pairs, last], axis=1).astype(BF16)

    def from_message(got):
        pairs, last = got[:, group : group + third], got[:, group + third :]
        lanes = lax.broadcasted_iota(jnp.int32, pairs.shape, 2)
        first = jnp.where(lanes < hd, pairs, pltpu.roll(last, BLOCK - 2, 2))
        second = jnp.where(lanes < hd, pltpu.roll(pairs, hd, 2), pltpu.roll(last, BLOCK - 4, 2))
        return got[:, :group], jnp.concatenate([first, second, last], axis=1)

    rows = 2 * batch * group

    def order_rows(g):
        index = (lax.broadcasted_iota(jnp.int32, (rows, rows_dev), 0) + g * rows).astype(F32)
        pick = jnp.where(index == place[...], 1.0, 0.0).astype(BF16)
        ordered = jnp.dot(pick, packed[...], preferred_element_type=F32)
        made = message(spread(ordered[:, :BLOCK]), spread(ordered[:, BLOCK:]))
        trade[g] = made[:batch]
        send[pl.ds(g * batch, batch), core] = made[batch:]

    def send_batch(g):
        core_trade(g).wait_recv()
        each(g * batch, min((g + 1) * batch, chips - 1), lambda j: exchange(j).start())

    for g in range(batches):
        order_rows(g)
        if g == 0:
            pl.semaphore_wait(barrier, chips - 1 + 2 + mp - 1)
        core_trade(g).start()
        if g > 0:
            send_batch(g - 1)
    send_batch(batches - 1)
    recv[chips - 1] = send[chips - 1]

    lane8 = lax.broadcasted_iota(jnp.int32, (8, BLOCK), 1)
    decode = jnp.where(lane8 == hd, 64.0, jnp.where(lane8 == hd + 1, 1.0, 0.0)).astype(BF16)
    per_tile = tile // BLOCK
    edges = [g * batch for g in range(batches)] + [chips - batch // 2] * (batch > 1) + [chips]
    centre = [i for n in range((tiles + 1) // 2) for i in dict.fromkeys((n, tiles - 1 - n))]
    for g, (start, stop) in enumerate(zip(edges, edges[1:])):
        each(start, min(stop, chips - 1), lambda j: exchange(j).wait_recv())
        rows = 2 * (stop - start) * group
        got = recv[start:stop].astype(F32)
        kv, q = from_message(got.reshape(-1, group + 2 * third, BLOCK))
        kv, q = kv.reshape(rows, BLOCK), q.reshape(rows, BLOCK)
        slot = lax.dot_general(decode, q.astype(BF16), NT, preferred_element_type=F32)[:1]
        got = jnp.concatenate([kv, q], axis=1).astype(BF16)
        for i in centre:
            part = pl.ds(i * tile, tile)
            index = (lax.broadcasted_iota(jnp.int32, (tile, rows), 0) + i * tile).astype(F32)
            pick = jnp.where(index == slot, 1.0, 0.0).astype(BF16)
            found = jnp.dot(pick, got, preferred_element_type=F32)
            if g > 0:
                found = acc[part] + found
            if stop < chips:
                acc[part] = found
            else:
                kv = found[:, :BLOCK].astype(BF16)
                q = jnp.where(lane < hd, found[:, BLOCK:], 0.0).astype(BF16)
                keyval[pl.ds(reach + i * per_tile, per_tile)] = kv.reshape(per_tile, BLOCK, BLOCK)
                query[pl.ds(i * per_tile, per_tile)] = q.reshape(per_tile, BLOCK, BLOCK)
                for copy in halo(i):
                    copy.start()
    for i in range(tiles):
        for copy in halo(i):
            copy.wait_recv()

    lane_half = lax.broadcasted_iota(jnp.int32, (BLOCK // 2, BLOCK), 1)

    def attend(b):
        kvs, absent = [], []
        for s in range(neigh):
            nb = nb_ref[b, s]
            at = nb - me * blocks + reach
            at = jnp.where(at < 0, at + nblk, jnp.where(at >= blocks + 2 * reach, at - nblk, at))
            kvs.append(keyval[jnp.clip(jnp.where(nb >= 0, at, 0), 0, blocks + 2 * reach - 1)])
            absent.append(jnp.where(nb >= 0, 0.0, -1e30))
        kvs = jnp.concatenate(kvs, axis=0)
        scores = lax.dot_general(query[b], kvs, NT, preferred_element_type=F32)
        cut = (neigh - MASKED) * BLOCK
        tail = [scores[:, s * BLOCK : (s + 1) * BLOCK] + absent[s] for s in range(neigh - MASKED, neigh)]
        scores = jnp.concatenate([scores[:, :cut], *tail], axis=1)
        weights = jnp.exp(scores - jnp.max(scores, axis=1, keepdims=True))
        total = jnp.sum(weights, axis=1, keepdims=True)
        values = jnp.dot(weights.astype(BF16), kvs, preferred_element_type=F32) / total
        half = BLOCK // 2
        return jnp.where(lane_half < hd, pltpu.roll(values[:half], hd, 1), values[half:]).astype(BF16)

    for t in range(0, mp, 2):
        blocks_now = [(step, attend(ring(step))) for step in (t, t + 1)]
        for step, rows_now in blocks_now:
            if step < mp - 1:
                attn[step] = rows_now
                output_copy(step).start()
            else:
                heads[head] = rows_now

    wout_copy.wait()
    for t in range(0, mp, 2):
        came = []
        for step in (t, t + 1):
            if step < mp - 1:
                output_copy(step).wait_recv()
            came.append(lax.rem(head + mp - far_static(mp, step), mp))
        low, high = (heads[h].astype(F32) for h in came)
        top = jnp.where(lane_half < hd, low, pltpu.roll(high, hd, 1))
        bottom = jnp.where(lane_half < hd, pltpu.roll(low, hd, 1), high)
        pair = jnp.concatenate([top, bottom], axis=0).astype(BF16)
        weight = jnp.concatenate([wout[pl.ds(pl.multiple_of(h * hd, hd), hd)] for h in came], axis=0)
        term = jnp.dot(pair, weight, preferred_element_type=F32)
        if t > 0:
            term = mixed[...] + term
        if t < mp - 2:
            mixed[...] = term
        else:
            out_ref[...] = term.astype(BF16)

    each(0, batches, lambda g: core_trade(g).wait_send())
    each(0, chips - 1, lambda j: exchange(j).wait_send())
    for i in range(tiles):
        for copy in halo(i):
            copy.wait_send()
    each(0, mp - 1, lambda t: output_copy(t).wait_send())


def per_device(reach, tokens, norm_gain, w_qkv, w_out, head_scale, cycle_to_nested, neighbours):
    space, mp = lax.axis_size("space"), lax.axis_size("mp")
    rows, width = tokens.shape
    group, blocks = rows // space, rows // BLOCK
    tiles = rows // min(256, rows)
    chips = space // 2
    batch = max(1, chips // 4)
    batches, message = chips // batch, group + 2 * (group // 3)
    vmem, smem, anywhere = (pl.BlockSpec(memory_space=m) for m in (pltpu.VMEM, pltpu.SMEM, pl.ANY))
    dma = pltpu.SemaphoreType.DMA
    return pl.pallas_call(
        functools.partial(kernel, (space, mp, reach)),
        out_shape=pltpu.VMEM((rows // mp, w_out.shape[1]), BF16),
        in_specs=[anywhere, vmem, vmem, anywhere, smem, vmem, smem],
        out_specs=vmem,
        scratch_shapes=[
            pltpu.VMEM(tokens.shape, BF16),
            pltpu.VMEM(w_out.shape, BF16),
            pltpu.VMEM((rows, 2 * BLOCK), BF16),
            pltpu.VMEM((1, rows), F32),
            pltpu.VMEM((batches, batch, message, BLOCK), BF16),
            pltpu.VMEM((chips, 2, message, BLOCK), BF16),
            pltpu.VMEM((chips, 2, message, BLOCK), BF16),
            pltpu.VMEM((rows, 2 * BLOCK), F32),
            pltpu.VMEM((blocks, BLOCK, BLOCK), BF16),
            pltpu.VMEM((blocks + 2 * reach, BLOCK, BLOCK), BF16),
            pltpu.VMEM((mp, BLOCK // 2, BLOCK), BF16),
            pltpu.VMEM((mp, BLOCK // 2, BLOCK), BF16),
            pltpu.VMEM((rows // mp, w_out.shape[1]), F32),
            dma((tiles,)), dma, dma((batches,)), dma((batches,)), dma((chips,)), dma((chips,)), dma((tiles, 2)), dma((tiles, 2)), dma((mp,)), dma((mp,)),
        ],
        compiler_params=pltpu.CompilerParams(collective_id=0, has_side_effects=True, vmem_limit_bytes=56 * 2**20),
    )(
        tokens, norm_gain.reshape(1, width), w_qkv.transpose(1, 2, 0).reshape(-1, width), w_out, head_scale,
        cycle_to_nested, neighbours,
    )


def solution(mesh, reach=REACH):
    placed = (P("space", None), P(), P(None, "mp", None), P(), P("mp"), P("space"), P("space", None))
    return jax.shard_map(
        functools.partial(per_device, reach), mesh=mesh, in_specs=placed, out_specs=P(("space", "mp"), None), check_vma=False
    )
```

```python
import functools
import jax
import jax.numpy as jnp
from jax import lax
from jax.experimental import pallas as pl
from jax.experimental.pallas import tpu as pltpu
from jax.sharding import PartitionSpec as P

BLOCK = 128
REACH = 6
MASKED = 2
F32 = jnp.float32
BF16 = jnp.bfloat16
MESH = pl.DeviceIdType.MESH
NT = (((1,), (1,)), ((), ()))


def far_static(size, step):
    if size % 2:
        return (step + 1) % size
    return size // 2 - 1 - step // 2 if step % 2 else size // 2 + step // 2


def chip_steps(nx, ny):
    xs = [far_static(nx, i) if nx > 1 else 0 for i in range(nx)]
    steps = [(dx, ny // 2) for dx in xs]
    same = [(dx, 0) for dx in xs if dx]
    for level in range(ny // 2 - 1, 0, -1):
        if level == 1:
            steps += same
        steps += [(dx, dy) for dx in xs for dy in (level, ny - level)]
    return (steps if ny > 2 else steps + same) + [(0, 0)]


def split_space(size):
    across = 4 if size == 64 else size // 4
    return across, size // 2 // across


def kernel(
    dims, tok_hbm, gain_ref, w_ref, wout_hbm, scale_ref, cyc_ref, nb_ref, out_ref,
    tok, wout, packed, place, trade, send, recv, acc, query, keyval, attn, heads, mixed,
    tok_sem, wout_sem, csem, drem, ssem, rsem, hsem, grem, asem, arem,
):
    space, mp, reach = dims
    nx, ny = split_space(space)
    rows_dev, width = tok_hbm.shape
    hd = w_ref.shape[0] // 3
    group = rows_dev // space
    blocks = rows_dev // BLOCK
    nblk = blocks * space
    neigh = nb_ref.shape[1]
    tile = min(256, rows_dev)
    tiles = rows_dev // tile
    chips = space // 2
    batch = max(1, chips // 4)
    batches = chips // batch
    third = group // 3

    me, head = lax.axis_index("space"), lax.axis_index("mp")
    core, my_y, my_x = lax.rem(me, 2), lax.rem(me // 2, ny), me // (2 * ny)
    steps = chip_steps(nx, ny)

    def displaced(j):
        dx, dy = steps[j]
        return lax.rem(my_x + dx, nx) * ny + lax.rem(my_y + dy, ny)

    def ring(t):
        return lax.rem(head + far_static(mp, t), mp)

    def token_copy(i):
        part = pl.ds(pl.multiple_of(i * tile, tile), tile)
        return pltpu.make_async_copy(tok_hbm.at[part], tok.at[part], tok_sem.at[i])

    def core_trade(g):
        return pltpu.make_async_remote_copy(
            src_ref=trade.at[g], dst_ref=send.at[pl.ds(g * batch, batch), core], send_sem=csem.at[g], recv_sem=drem.at[g],
            device_id=(me + 1 - 2 * core, head), device_id_type=MESH,
        )

    def exchange(j):
        return pltpu.make_async_remote_copy(
            src_ref=send.at[j], dst_ref=recv.at[j], send_sem=ssem.at[j], recv_sem=rsem.at[j],
            device_id=(displaced(j) * 2 + core, head), device_id_type=MESH,
        )

    def halo(i):
        per_tile = tile // BLOCK
        low, high = i * per_tile, (i + 1) * per_tile
        pieces = []
        if low < reach:
            pieces.append((low, min(high, reach) - low, low + reach + blocks, me + space - 1))
        if high > blocks - reach:
            first = max(low, blocks - reach)
            pieces.append((first, high - first, first - (blocks - reach), me + 1))
        return [
            pltpu.make_async_remote_copy(
                src_ref=keyval.at[pl.ds(reach + start, count)], dst_ref=keyval.at[pl.ds(to, count)],
                send_sem=hsem.at[i, n], recv_sem=grem.at[i, n], device_id=(who % space, head), device_id_type=MESH,
            )
            for n, (start, count, to, who) in enumerate(pieces)
        ]

    def output_copy(t):
        return pltpu.make_async_remote_copy(
            src_ref=attn.at[t], dst_ref=heads.at[head], send_sem=asem.at[t], recv_sem=arem.at[t],
            device_id=(me, ring(t)), device_id_type=MESH,
        )

    def each(start, stop, body):
        for i in range(start, stop):
            body(i)

    barrier = pltpu.get_barrier_semaphore()
    each(0, chips - 1, lambda j: pl.semaphore_signal(barrier, inc=1, device_id=(displaced(j) * 2 + core, head), device_id_type=MESH))
    pl.semaphore_signal(barrier, inc=1, device_id=((me + 1) % space, head), device_id_type=MESH)
    pl.semaphore_signal(barrier, inc=1, device_id=((me + space - 1) % space, head), device_id_type=MESH)
    each(0, mp - 1, lambda t: pl.semaphore_signal(barrier, inc=1, device_id=(me, ring(t)), device_id_type=MESH))

    each(0, tiles, lambda i: token_copy(i).start())
    wout_copy = pltpu.make_async_copy(wout_hbm, wout, wout_sem)
    wout_copy.start()

    step_ids = lax.broadcasted_iota(jnp.int32, (space, tile), 0)
    targets = jnp.zeros_like(step_ids)
    for j in range(chips):
        start = j // batch * 2 * batch + j % batch
        chip = displaced(j) * 2
        targets = jnp.where(step_ids == start, chip + 1 - core, jnp.where(step_ids == start + batch, chip + core, targets))
    before = jnp.where(
        lax.broadcasted_iota(jnp.int32, (tile, tile), 0) < lax.broadcasted_iota(jnp.int32, (tile, tile), 1), 1.0, 0.0
    ).astype(BF16)
    offset = step_ids.astype(F32) * group
    for i in range(tiles):
        cyc = cyc_ref[pl.ds(i * tile, tile)].reshape(1, tile).astype(F32)
        owner = jnp.floor((cyc + 0.5) * (1.0 / rows_dev)).astype(jnp.int32)
        chosen = jnp.where(targets == owner, 1.0, 0.0)
        ahead = jnp.dot(chosen.astype(BF16), before, preferred_element_type=F32) + offset
        place[:, i * tile : (i + 1) * tile] = jnp.sum(chosen * ahead, axis=0, keepdims=True)
        offset = offset + jnp.sum(chosen, axis=1, keepdims=True)

    weight = w_ref[...]
    weight = jnp.concatenate([weight[hd:], weight[:hd], jnp.zeros((2 * BLOCK - 3 * hd, width), BF16)], axis=0)
    lane = lax.broadcasted_iota(jnp.int32, (tile, BLOCK), 1)
    gain = gain_ref[...]
    scale = scale_ref[0]

    def project(i):
        token_copy(i).wait()
        part = pl.ds(pl.multiple_of(i * tile, tile), tile)
        values = tok[part].astype(F32)
        mean_square = jnp.mean(values * values, axis=1, keepdims=True)
        normed = (values * lax.rsqrt(mean_square + 1e-05) * gain).astype(BF16)
        projected = lax.dot_general(normed, weight, NT, preferred_element_type=F32)
        kv, q = projected[:, :BLOCK], projected[:, BLOCK:]
        key_square = jnp.sum(jnp.where(lane < hd, kv * kv, 0.0), axis=1, keepdims=True)
        kv = kv * jnp.where(lane < hd, lax.rsqrt(key_square + 1e-06), 1.0)
        q = q * (scale * lax.rsqrt(jnp.sum(q * q, axis=1, keepdims=True) + 1e-06))
        cyc = cyc_ref[part].reshape(1, tile).astype(F32)
        cyc = jnp.concatenate(
            [jnp.broadcast_to(cyc[:, r : r + BLOCK], (BLOCK, BLOCK)).T for r in range(0, tile, BLOCK)], axis=0
        )
        slot = cyc - rows_dev * jnp.floor((cyc + 0.5) * (1.0 / rows_dev))
        upper = jnp.floor(slot * (1.0 / 64))
        q = jnp.where(lane == hd, upper, jnp.where(lane == hd + 1, slot - 64 * upper, q))
        packed[part] = jnp.concatenate([kv, q], axis=1).astype(BF16)

    lax.fori_loop(0, tiles, lambda i, carry: (project(i), carry)[1], 0)

    def spread(values):
        return values.reshape(-1, group, BLOCK)

    def message(kv, q):
        first, second, last = q[:, :third], q[:, third : 2 * third], q[:, 2 * third :]
        lanes = lax.broadcasted_iota(jnp.int32, first.shape, 2)
        pairs = jnp.where(lanes < hd, first, pltpu.roll(second, hd, 2))
        last = jnp.where((lanes == hd + 2) | (lanes == hd + 3), pltpu.roll(first, 2, 2), last)
        last = jnp.where((lanes == hd + 4) | (lanes == hd + 5), pltpu.roll(second, 4, 2), last)
        return jnp.concatenate([kv, pairs, last], axis=1).astype(BF16)

    def from_message(got):
        pairs, last = got[:, group : group + third], got[:, group + third :]
        lanes = lax.broadcasted_iota(jnp.int32, pairs.shape, 2)
        first = jnp.where(lanes < hd, pairs, pltpu.roll(last, BLOCK - 2, 2))
        second = jnp.where(lanes < hd, pltpu.roll(pairs, hd, 2), pltpu.roll(last, BLOCK - 4, 2))
        return got[:, :group], jnp.concatenate([first, second, last], axis=1)

    rows = 2 * batch * group

    def order_rows(g):
        index = (lax.broadcasted_iota(jnp.int32, (rows, rows_dev), 0) + g * rows).astype(F32)
        pick = jnp.where(index == place[...], 1.0, 0.0).astype(BF16)
        ordered = jnp.dot(pick, packed[...], preferred_element_type=F32)
        made = message(spread(ordered[:, :BLOCK]), spread(ordered[:, BLOCK:]))
        trade[g] = made[:batch]
        send[pl.ds(g * batch, batch), core] = made[batch:]

    def send_batch(g):
        core_trade(g).wait_recv()
        each(g * batch, min((g + 1) * batch, chips - 1), lambda j: exchange(j).start())

    for g in range(batches):
        order_rows(g)
        if g == 0:
            pl.semaphore_wait(barrier, chips - 1 + 2 + mp - 1)
        core_trade(g).start()
        if g > 0:
            send_batch(g - 1)
    send_batch(batches - 1)
    recv[chips - 1] = send[chips - 1]

    lane8 = lax.broadcasted_iota(jnp.int32, (8, BLOCK), 1)
    decode = jnp.where(lane8 == hd, 64.0, jnp.where(lane8 == hd + 1, 1.0, 0.0)).astype(BF16)
    per_tile = tile // BLOCK
    edges = [g * batch for g in range(batches)] + [chips - batch // 2] * (batch > 1) + [chips]
    centre = [i for n in range((tiles + 1) // 2) for i in dict.fromkeys((n, tiles - 1 - n))]
    for g, (start, stop) in enumerate(zip(edges, edges[1:])):
        each(start, min(stop, chips - 1), lambda j: exchange(j).wait_recv())
        rows = 2 * (stop - start) * group
        got = recv[start:stop].astype(F32)
        kv, q = from_message(got.reshape(-1, group + 2 * third, BLOCK))
        kv, q = kv.reshape(rows, BLOCK), q.reshape(rows, BLOCK)
        slot = lax.dot_general(decode, q.astype(BF16), NT, preferred_element_type=F32)[:1]
        got = jnp.concatenate([kv, q], axis=1).astype(BF16)
        for i in centre:
            part = pl.ds(i * tile, tile)
            index = (lax.broadcasted_iota(jnp.int32, (tile, rows), 0) + i * tile).astype(F32)
            pick = jnp.where(index == slot, 1.0, 0.0).astype(BF16)
            found = jnp.dot(pick, got, preferred_element_type=F32)
            if g > 0:
                found = acc[part] + found
            if stop < chips:
                acc[part] = found
            else:
                kv = found[:, :BLOCK].astype(BF16)
                q = jnp.where(lane < hd, found[:, BLOCK:], 0.0).astype(BF16)
                keyval[pl.ds(reach + i * per_tile, per_tile)] = kv.reshape(per_tile, BLOCK, BLOCK)
                query[pl.ds(i * per_tile, per_tile)] = q.reshape(per_tile, BLOCK, BLOCK)
                for copy in halo(i):
                    copy.start()
    for i in range(tiles):
        for copy in halo(i):
            copy.wait_recv()

    lane_half = lax.broadcasted_iota(jnp.int32, (BLOCK // 2, BLOCK), 1)

    def attend(b):
        kvs, absent = [], []
        for s in range(neigh):
            nb = nb_ref[b, s]
            at = nb - me * blocks + reach
            at = jnp.where(at < 0, at + nblk, jnp.where(at >= blocks + 2 * reach, at - nblk, at))
            kvs.append(keyval[jnp.clip(jnp.where(nb >= 0, at, 0), 0, blocks + 2 * reach - 1)])
            absent.append(jnp.where(nb >= 0, 0.0, -1e30))
        kvs = jnp.concatenate(kvs, axis=0)
        scores = lax.dot_general(query[b], kvs, NT, preferred_element_type=F32)
        cut = (neigh - MASKED) * BLOCK
        tail = [scores[:, s * BLOCK : (s + 1) * BLOCK] + absent[s] for s in range(neigh - MASKED, neigh)]
        scores = jnp.concatenate([scores[:, :cut], *tail], axis=1)
        weights = jnp.exp(scores - jnp.max(scores, axis=1, keepdims=True))
        total = jnp.sum(weights, axis=1, keepdims=True)
        values = jnp.dot(weights.astype(BF16), kvs, preferred_element_type=F32) / total
        half = BLOCK // 2
        return jnp.where(lane_half < hd, pltpu.roll(values[:half], hd, 1), values[half:]).astype(BF16)

    for t in range(0, mp, 2):
        blocks_now = [(step, attend(ring(step))) for step in (t, t + 1)]
        for step, rows_now in blocks_now:
            if step < mp - 1:
                attn[step] = rows_now
                output_copy(step).start()
            else:
                heads[head] = rows_now

    wout_copy.wait()
    each(0, batches, lambda g: core_trade(g).wait_send())
    each(0, chips - 1, lambda j: exchange(j).wait_send())
    for i in range(tiles):
        for copy in halo(i):
            copy.wait_send()
    for t in range(0, mp, 2):
        came = []
        for step in (t, t + 1):
            if step < mp - 1:
                output_copy(step).wait_recv()
            came.append(lax.rem(head + mp - far_static(mp, step), mp))
        low, high = (heads[h].astype(F32) for h in came)
        top = jnp.where(lane_half < hd, low, pltpu.roll(high, hd, 1))
        bottom = jnp.where(lane_half < hd, pltpu.roll(low, hd, 1), high)
        pair = jnp.concatenate([top, bottom], axis=0).astype(BF16)
        weight = jnp.concatenate([wout[pl.ds(pl.multiple_of(h * hd, hd), hd)] for h in came], axis=0)
        term = jnp.dot(pair, weight, preferred_element_type=F32)
        if t > 0:
            term = mixed[...] + term
        if t < mp - 2:
            mixed[...] = term
        else:
            out_ref[...] = term.astype(BF16)

    each(0, mp - 1, lambda t: output_copy(t).wait_send())


def per_device(reach, tokens, norm_gain, w_qkv, w_out, head_scale, cycle_to_nested, neighbours):
    space, mp = lax.axis_size("space"), lax.axis_size("mp")
    rows, width = tokens.shape
    group, blocks = rows // space, rows // BLOCK
    tiles = rows // min(256, rows)
    chips = space // 2
    batch = max(1, chips // 4)
    batches, message = chips // batch, group + 2 * (group // 3)
    vmem, smem, anywhere = (pl.BlockSpec(memory_space=m) for m in (pltpu.VMEM, pltpu.SMEM, pl.ANY))
    dma = pltpu.SemaphoreType.DMA
    return pl.pallas_call(
        functools.partial(kernel, (space, mp, reach)),
        out_shape=pltpu.VMEM((rows // mp, w_out.shape[1]), BF16),
        in_specs=[anywhere, vmem, vmem, anywhere, smem, vmem, smem],
        out_specs=vmem,
        scratch_shapes=[
            pltpu.VMEM(tokens.shape, BF16),
            pltpu.VMEM(w_out.shape, BF16),
            pltpu.VMEM((rows, 2 * BLOCK), BF16),
            pltpu.VMEM((1, rows), F32),
            pltpu.VMEM((batches, batch, message, BLOCK), BF16),
            pltpu.VMEM((chips, 2, message, BLOCK), BF16),
            pltpu.VMEM((chips, 2, message, BLOCK), BF16),
            pltpu.VMEM((rows, 2 * BLOCK), F32),
            pltpu.VMEM((blocks, BLOCK, BLOCK), BF16),
            pltpu.VMEM((blocks + 2 * reach, BLOCK, BLOCK), BF16),
            pltpu.VMEM((mp, BLOCK // 2, BLOCK), BF16),
            pltpu.VMEM((mp, BLOCK // 2, BLOCK), BF16),
            pltpu.VMEM((rows // mp, w_out.shape[1]), F32),
            dma((tiles,)), dma, dma((batches,)), dma((batches,)), dma((chips,)), dma((chips,)), dma((tiles, 2)), dma((tiles, 2)), dma((mp,)), dma((mp,)),
        ],
        compiler_params=pltpu.CompilerParams(collective_id=0, has_side_effects=True, vmem_limit_bytes=56 * 2**20),
    )(
        tokens, norm_gain.reshape(1, width), w_qkv.transpose(1, 2, 0).reshape(-1, width), w_out, head_scale,
        cycle_to_nested, neighbours,
    )


def solution(mesh, reach=REACH):
    placed = (P("space", None), P(), P(None, "mp", None), P(), P("mp"), P("space"), P("space", None))
    return jax.shard_map(
        functools.partial(per_device, reach), mesh=mesh, in_specs=placed, out_specs=P(("space", "mp"), None), check_vma=False
    )
```
